32 devices in a mesh: groups: 2 (over y), space: 8 (over z, x), seg: 2 (over core).
Axes of the slice: x: 2, y: 2, z: 4, core: 2. Of those that a mesh axis runs over, the one named last changes fastest.
Arguments:
- modes: bfloat16 [8, 32, 128, 128], P(None, 'space'), may hold values from -0.1 to 0.1
- states: float32 [32, 8, 32, 128], P(('groups', 'seg'), None, 'space'), parts along dimension 0, may hold values from -6 to 6
- lift_one: bfloat16 [64, 8], replicated, may hold values from -2 to 2
- kern_one: float32 [64, 9], replicated, may hold values from -2 to 2
- bias_one: float32 [64], replicated, may hold values from -3 to 3
- proj_one: bfloat16 [8, 64], replicated, may hold values from -0.75 to 0.75
- lift_two: bfloat16 [64, 8], replicated, may hold values from -2 to 2
- kern_two: float32 [64, 9], replicated, may hold values from -2 to 2
- bias_two: float32 [64], replicated, may hold values from -3 to 3
- proj_two: bfloat16 [8, 64], replicated, may hold values from -0.75 to 0.75
Outputs:
- advanced: float32 [32, 8, 32, 128], P(('groups', 'seg'), None, 'space'), parts along dimension 0
- coeffs: float32 [32, 128], P(('groups', 'seg')), parts along dimension 0
The draws below stay inside these ranges and needn't reach their ends.
There are 2 independent parts, one for each index of `groups`. The reference program is written for one: setup_inputs(seed, part) draws one part's arguments, and reference() takes and returns one part's arrays. A program takes and returns all parts, laid end to end along the dimension named above; an argument that names none is the same for every part. Nothing has to cross between parts.
All inputs are finite; a program needn't handle non-finite values.
Results may differ from the reference program's by a relative error of at most 0.0033.
Values may be sent and summed in bfloat16 or wider, within the bound.
A program may use at most 320 MiB of HBM per device.

```python
import jax
import jax.numpy as jnp
from jax import lax

FIELDS = 8
CH = 64
MODES = 128
COLS = 128
ROWS = 32
SEGMENTS = 16


def draw_modes(key, part):
    base = jax.random.fold_in(key, 11)
    first, second = jax.random.split(base)
    shape = (FIELDS, ROWS, COLS, MODES)
    noise = jax.random.normal(first, shape, jnp.float32)
    noise = noise / jnp.sqrt(jnp.float32(FIELDS * ROWS * COLS))
    mixing = jnp.eye(MODES, dtype=jnp.float32) + 0.25 * jax.random.normal(second, (MODES, MODES), jnp.float32) / jnp.sqrt(jnp.float32(MODES))
    mixed = 0.7 * jnp.einsum('frwk,kj->frwj', noise, mixing)
    return jnp.clip(mixed, -0.099, 0.099).astype(jnp.bfloat16)


def level_of(stream_key, extent, cuts, low, high):
    factor_of = 1.0
    for dim, blocks in cuts:
        draws = jax.random.uniform(jax.random.fold_in(jax.random.fold_in(stream_key, 6), dim), (blocks,), jnp.float32, low / len(cuts), high / len(cuts))
        factor_of = factor_of * jnp.repeat(jnp.exp(draws), extent[dim] // blocks).reshape((-1,) + (1,) * (len(extent) - 1 - dim))
    return factor_of


def gaussian(key, dims, width, bound, cuts=(), kind=jnp.bfloat16):
    drawn = width * jax.random.normal(key, dims, jnp.float32)
    if cuts:
        drawn = drawn * level_of(key, dims, cuts, -0.22, 0.18)
    return jnp.clip(drawn, -bound, bound).astype(kind)


def setup_inputs(seed: int = 0, part: int = 0) -> dict:
    streams_of = jax.random.split(jax.random.key(seed), 11)
    part_splits = jax.random.split(jax.random.fold_in(streams_of[10], part), 11)
    return {
        "modes": draw_modes(jax.random.fold_in(streams_of[10], 71), part),
        "states": gaussian(part_splits[1], (SEGMENTS, FIELDS, ROWS, COLS), 1.0, 6.0, ((0, 2), (2, 8)), jnp.float32),
        "lift_one": gaussian(streams_of[2], (CH, FIELDS), FIELDS ** -0.5, 2.0),
        "kern_one": gaussian(streams_of[3], (CH, 9), 9 ** -0.5, 2.0, (), jnp.float32),
        "bias_one": gaussian(streams_of[4], (CH,), 0.5, 3.0, (), jnp.float32),
        "proj_one": gaussian(streams_of[5], (FIELDS, CH), CH ** -0.5, 0.75),
        "lift_two": gaussian(streams_of[6], (CH, FIELDS), FIELDS ** -0.5, 2.0),
        "kern_two": gaussian(streams_of[7], (CH, 9), 9 ** -0.5, 2.0, (), jnp.float32),
        "bias_two": gaussian(streams_of[8], (CH,), 0.5, 3.0, (), jnp.float32),
        "proj_two": gaussian(streams_of[9], (FIELDS, CH), CH ** -0.5, 0.75),
    }


HI = lax.Precision.HIGHEST


def depthwise(z, kern):
    r, w = z.shape[1], z.shape[2]
    pads = [(0, 0), (1, 1), (1, 1)] + [(0, 0)] * (z.ndim - 3)
    padded = jnp.pad(z, pads)
    total = jnp.zeros(z.shape, jnp.float32)
    for i in range(3):
        for j in range(3):
            weight = kern[:, 3 * i + j].reshape((-1,) + (1,) * (z.ndim - 1))
            total = total + weight * padded[:, i:i + r, j:j + w]
    return total


def advance(field, lift, kern, bias, proj):
    lifted = jnp.einsum('cf,frw->crw', lift.astype(jnp.float32), field, precision=HI)
    act = jnp.tanh(depthwise(lifted, kern) + bias[:, None, None])
    out = field + jnp.einsum('fc,crw->frw', proj.astype(jnp.float32), act, precision=HI)
    return out, 1.0 - act * act


def tangent_block(inputs, slope, lift, kern, proj):
    lifted = jnp.einsum('cf,frwk->crwk', lift.astype(jnp.float32), inputs.astype(jnp.float32))
    scaled = (slope[..., None] * depthwise(lifted, kern)).astype(jnp.bfloat16)
    mixed = jnp.einsum('fc,crwk->frwk', proj.astype(jnp.float32), scaled.astype(jnp.float32))
    return (inputs.astype(jnp.float32) + mixed).astype(jnp.bfloat16)


def reference(modes, states, lift_one, kern_one, bias_one, proj_one, lift_two, kern_two, bias_two, proj_two):
    fields, rows, cols, nmodes = modes.shape
    blocks = modes.reshape(fields, rows, cols, nmodes // 8, 8).transpose(3, 0, 1, 2, 4)
    advanced = []
    coeffs = []
    current = jnp.zeros((nmodes,), jnp.float32)
    for seg in range(SEGMENTS):
        middle, slope_one = advance(states[seg], lift_one, kern_one, bias_one, proj_one)
        final, slope_two = advance(middle, lift_two, kern_two, bias_two, proj_two)
        advanced.append(final)
        coeffs.append(current)
        if seg < SEGMENTS - 1:
            def tangent(block):
                first = tangent_block(block, slope_one, lift_one, kern_one, proj_one)
                return tangent_block(first, slope_two, lift_two, kern_two, proj_two)
            result = lax.map(tangent, blocks)
            result = result.transpose(1, 2, 3, 0, 4).reshape(fields, rows, cols, nmodes)
            matrix = jnp.einsum('frwi,frwj->ij', modes.astype(jnp.float32), result.astype(jnp.float32))
            defect = (final - states[seg + 1]).astype(jnp.bfloat16)
            shift_vec = jnp.einsum('frwk,frw->k', modes.astype(jnp.float32), defect.astype(jnp.float32))
            current = jnp.dot(matrix, current, precision=HI) + shift_vec
    return jnp.stack(advanced), jnp.stack(coeffs)
```

```python
import functools

import jax
import jax.numpy as jnp
import numpy as np
from jax import lax
from jax.experimental import pallas as pl
from jax.experimental.pallas import tpu as pltpu
from jax.sharding import PartitionSpec as P

HI = lax.Precision.HIGHEST
F32 = jnp.float32
BF16 = jnp.bfloat16


def dot(a, b):
    return jnp.dot(a, b, preferred_element_type=F32)


def dot_split(x, weight):
    high = x.astype(BF16)
    low = (x - high.astype(F32)).astype(BF16)
    return dot(high, weight) + dot(low, weight)


def regroup(x):
    x = x.reshape(4, 4, 8, 64)
    return jnp.concatenate([x[:, a] for a in range(4)], axis=-1)


def advance_kernel(
    rows, mask_ref, u_ref, l1, l2, p1, p2, k1, k2, b1, b2, s1_ref, s2_ref, out_ref, z_ref, z2_ref, m_ref
):
    span = u_ref.shape[1]
    edge1 = jnp.zeros((rows + 4, 8, z_ref.shape[2]), F32)
    edge2 = jnp.zeros((rows + 2, 8, z_ref.shape[2]), F32)
    z_ref[:, 0:8, :] = edge1
    z_ref[:, span + 8 : span + 16, :] = edge1
    z2_ref[:, 0:8, :] = edge2
    z2_ref[:, span + 8 : span + 16, :] = edge2

    @pl.loop(0, rows + 4)
    def _(r):
        z_ref[r, 8 : span + 8, :] = dot_split(u_ref[r], l1[...])

    pieces = span // 128

    def conv(ref, taps, bias, r, base):
        acc = jnp.broadcast_to(bias[...], (128, taps.shape[1]))
        for i in range(3):
            for j in range(3):
                acc = acc + taps[3 * i + j : 3 * i + j + 1, :] * ref[r + i, pl.ds(base + 8 * j, 128), :]
        return jnp.tanh(acc)

    @pl.loop(0, (rows + 2) * pieces)
    def _(n):
        r, q = n // pieces, n % pieces
        base = pl.multiple_of(q * 128, 128)
        keep = mask_ref[r]
        act = conv(z_ref, k1, b1, r, base)
        s1_ref[r, pl.ds(q * 4, 4)] = regroup((1.0 - act * act) * keep)
        mid = (u_ref[r + 1, pl.ds(base, 128), :] + dot_split(act, p1[...])) * keep
        m_ref[r, pl.ds(base, 128), :] = mid
        z2_ref[r, pl.ds(base + 8, 128), :] = dot_split(mid, l2[...])

    @pl.loop(0, rows * pieces)
    def _(n):
        r, q = n // pieces, n % pieces
        base = pl.multiple_of(q * 128, 128)
        act = conv(z2_ref, k2, b2, r, base)
        s2_ref[r, pl.ds(q * 4, 4)] = regroup(1.0 - act * act)
        out_ref[r, pl.ds(base, 128), :] = m_ref[r + 1, pl.ds(base, 128), :] + dot_split(act, p2[...])


def tangent_kernel(
    rows, segs, low_ref, own_ref, high_ref, turned_ref, s1_ref, s2_ref, pd1, pd2, kern1, kern2, lift1, lift2,
    sel_ref, rep_ref, maps_ref, x_ref, v_ref, t_ref, k1_ref, k2_ref,
):
    span = turned_ref.shape[2]
    tiles = span // 64
    nm = own_ref.shape[2]
    x_ref[0:2] = low_ref[...]
    x_ref[2 : rows + 2] = own_ref[...]
    x_ref[rows + 2 : rows + 4] = high_ref[...]
    v_ref[:, 0:8, :] = jnp.zeros((rows + 2, 8, segs * nm), F32)
    v_ref[:, span + 8 : span + 32, :] = jnp.zeros((rows + 2, 24, segs * nm), F32)
    for kern, lift, k_ref in ((kern1, lift1, k1_ref), (kern2, lift2, k2_ref)):
        wide = jnp.dot(lift[...].astype(F32), rep_ref[...], precision=HI, preferred_element_type=F32)
        for col in range(8):
            taps = jnp.dot(kern[...], sel_ref[col], precision=HI, preferred_element_type=F32)
            k_ref[col // 4, (col % 4) * 64 : (col % 4 + 1) * 64, :] = (taps * wide).astype(BF16)
    maps_ref[...] = jnp.zeros_like(maps_ref)

    def band(slopes, pd, k_ref, h):
        scale = pd[...]
        lhs = jnp.concatenate([(slopes[s : s + 1, :] * scale).astype(BF16) for s in range(segs)], axis=0)
        return dot(lhs, k_ref[h]).astype(BF16)

    @pl.loop(0, (rows + 2) * tiles)
    def _(n):
        r, t = n // tiles, n % tiles
        at = pl.multiple_of(t * 64, 64)
        middle = x_ref[r + 1, pl.ds(at, 80), :]
        near = jnp.concatenate([x_ref[r, pl.ds(at, 80), :], middle, x_ref[r + 2, pl.ds(at, 96), :]], axis=0)
        middle = middle.astype(F32)
        for h in range(2):
            out = dot(band(s1_ref[r, 2 * t + h], pd1, k1_ref, h), near)
            own = middle[8 + 32 * h : 40 + 32 * h]
            for s in range(segs):
                v_ref[r, pl.ds(at + (8 + 32 * h), 32), s * nm : (s + 1) * nm] = own + out[s * 32 : (s + 1) * 32]

    @pl.loop(0, rows)
    def _(r):
        @pl.loop(0, tiles)
        def _(t):
            at = pl.multiple_of(t * 64, 64)
            bands = [band(s2_ref[r, 2 * t + h], pd2, k2_ref, h) for h in range(2)]
            for s in range(segs):
                lanes = slice(s * nm, (s + 1) * nm)
                middle = v_ref[r + 1, pl.ds(at, 80), lanes].astype(BF16)
                near = jnp.concatenate(
                    [
                        v_ref[r, pl.ds(at, 80), lanes].astype(BF16),
                        middle,
                        v_ref[r + 2, pl.ds(at, 96), lanes].astype(BF16),
                    ],
                    axis=0,
                )
                both = jnp.concatenate([b[s * 32 : (s + 1) * 32] for b in bands], axis=0)
                out = dot(both, near) + middle.astype(F32)[8:72]
                t_ref[pl.ds(at, 64), lanes] = out.astype(BF16)

        maps_ref[...] += dot(turned_ref[r], t_ref[...])


def chain_kernel(segs, mats_ref, vecs_ref, start_ref, coeffs_ref, end_ref):
    nm = mats_ref.shape[0]
    current = start_ref[...]
    for s in range(segs):
        coeffs_ref[s : s + 1, :] = current[0:1, :]
        current = (
            lax.dot_general(
                current, mats_ref[:, s * nm : (s + 1) * nm], (((1,), (1,)), ((), ())),
                precision=HI, preferred_element_type=F32,
            )
            + vecs_ref[s : s + 1, :]
        )
    end_ref[...] = current


def selectors():
    sel = np.zeros((8, 9, 256), np.float32)
    rep = np.zeros((8, 256), np.float32)
    for i in range(3):
        for w in range(10):
            for g in range(8):
                lane = 80 * i + 8 * w + g
                rep[g, lane] = 1.0
                for col in range(8):
                    if 0 <= w - col < 3:
                        sel[col, 3 * i + w - col, lane] = 1.0
    return sel, rep


VM = pl.BlockSpec(memory_space=pltpu.VMEM)
SM = pl.BlockSpec(memory_space=pltpu.SMEM)


def on_device(
    modes, states, lift_one, kern_one, bias_one, proj_one, lift_two, kern_two, bias_two, proj_two
):
    fields, rows, cols, nmodes = modes.shape
    segs = states.shape[0]
    channels = lift_one.shape[0]
    count = lax.axis_size("space")
    down = [(i, i + 1) for i in range(count - 1)]
    up = [(i + 1, i) for i in range(count - 1)]

    before = lax.ppermute(states[:, :, rows - 2 :], "space", down)
    after = lax.ppermute(states[:, :, :2], "space", up)
    turns = lax.axis_size("seg")
    follow = lax.ppermute(states[0], "seg", [(i + 1, i) for i in range(turns - 1)])

    own = jnp.transpose(modes, (1, 2, 0, 3)).reshape(rows, cols * fields, nmodes)
    turned = jnp.transpose(own, (0, 2, 1))
    own = jnp.pad(own, ((0, 0), (8, 24), (0, 0)))
    low = lax.ppermute(own[rows - 2 :], "space", down)
    high = lax.ppermute(own[:2], "space", up)

    extended = jnp.concatenate([before, states, after], axis=2)
    u = jnp.transpose(extended, (2, 3, 0, 1)).reshape(rows + 4, cols * segs, fields)
    glob = lax.axis_index("space") * rows - 1 + jnp.arange(rows + 2)
    mask = ((glob >= 0) & (glob < rows * count)).astype(F32)

    groups = cols // 4
    span = cols * segs
    slope_one, slope_two, final = pl.pallas_call(
        functools.partial(advance_kernel, rows),
        out_shape=(
            jax.ShapeDtypeStruct((rows + 2, groups, segs, 4 * channels), F32),
            jax.ShapeDtypeStruct((rows, groups, segs, 4 * channels), F32),
            jax.ShapeDtypeStruct((rows, span, fields), F32),
        ),
        in_specs=[SM] + [VM] * 9,
        out_specs=(VM, VM, VM),
        scratch_shapes=[
            pltpu.VMEM((rows + 4, span + 16, channels), F32),
            pltpu.VMEM((rows + 2, span + 16, channels), F32),
            pltpu.VMEM((rows + 2, span, fields), F32),
        ],
        compiler_params=pltpu.CompilerParams(vmem_limit_bytes=56 * 2**20),
        cost_estimate=pl.CostEstimate(flops=10**8, bytes_accessed=10**7, transcendentals=10**6),
    )(
        mask, u, lift_one.T, lift_two.T, proj_one.T, proj_two.T, kern_one.T, kern_two.T,
        bias_one[None], bias_two[None],
    )
    advanced = jnp.transpose(final.reshape(rows, cols, segs, fields), (2, 3, 0, 1))
    defects = (advanced - jnp.concatenate([states[1:], follow[None]], axis=0)).astype(BF16)
    vecs = jnp.einsum("sfrw,frwk->sk", defects, modes, preferred_element_type=F32)

    sel, rep = selectors()
    blockwise = np.kron(np.eye(4, dtype=np.float32), np.ones((fields, channels), np.float32))
    pd1 = jnp.tile(proj_one.astype(F32), (4, 4)) * blockwise
    pd2 = jnp.tile(proj_two.astype(F32), (4, 4)) * blockwise
    lines = cols * fields
    mats = pl.pallas_call(
        functools.partial(tangent_kernel, rows, segs),
        out_shape=jax.ShapeDtypeStruct((nmodes, segs * nmodes), F32),
        in_specs=[VM] * 14,
        out_specs=VM,
        scratch_shapes=[
            pltpu.VMEM((rows + 4, lines + 32, nmodes), BF16),
            pltpu.VMEM((rows + 2, lines + 32, segs * nmodes), F32),
            pltpu.VMEM((lines, segs * nmodes), BF16),
            pltpu.VMEM((2, 256, 256), BF16),
            pltpu.VMEM((2, 256, 256), BF16),
        ],
        compiler_params=pltpu.CompilerParams(vmem_limit_bytes=56 * 2**20),
        cost_estimate=pl.CostEstimate(flops=2 * 10**10, bytes_accessed=10**7, transcendentals=0),
    )(
        low, own, high, turned, slope_one, slope_two, pd1, pd2, kern_one, kern_two, lift_one, lift_two, sel, rep
    )

    mats, vecs = lax.psum((mats, vecs), "space")
    chain = pl.pallas_call(
        functools.partial(chain_kernel, segs),
        out_shape=(
            jax.ShapeDtypeStruct((segs, nmodes), F32),
            jax.ShapeDtypeStruct((8, nmodes), F32),
        ),
        in_specs=[VM] * 3,
        out_specs=(VM, VM),
    )
    start = jnp.zeros((8, nmodes), F32)
    for _ in range(turns - 1):
        end = chain(mats, vecs, start)[1]
        start = lax.ppermute(end, "seg", [(i, i + 1) for i in range(turns - 1)])
    coeffs = chain(mats, vecs, start)[0]
    return advanced, coeffs


def solution(mesh):
    placed = (
        P(None, "space", None, None),
        P(("groups", "seg"), None, "space", None),
        P(), P(), P(), P(), P(), P(), P(), P(),
    )
    return jax.shard_map(
        on_device,
        mesh=mesh,
        in_specs=placed,
        out_specs=(P(("groups", "seg"), None, "space", None), P(("groups", "seg"), None)),
        check_vma=False,
    )
```

```python
import functools

import jax
import jax.numpy as jnp
import numpy as np
from jax import lax
from jax.experimental import pallas as pl
from jax.experimental.pallas import tpu as pltpu
from jax.sharding import PartitionSpec as P

HI = lax.Precision.HIGHEST
F32 = jnp.float32
BF16 = jnp.bfloat16


def dot(a, b):
    return jnp.dot(a, b, preferred_element_type=F32)


def dot_turned(a, b, side, precision=None):
    return lax.dot_general(
        a, b, (((side,), (side,)), ((), ())), precision=precision, preferred_element_type=F32
    )


def dot_split(x, weight, turned=False):
    high = x.astype(BF16)
    low = (x - high.astype(F32)).astype(BF16)
    if turned:
        return dot_turned(high, weight, 1) + dot_turned(low, weight, 1)
    return dot(high, weight) + dot(low, weight)


def regroup(x):
    x = x.reshape(x.shape[0] // 32, 4, 8, x.shape[1])
    return jnp.concatenate([x[:, a] for a in range(4)], axis=-1)


def advance_kernel(
    rows, mask_ref, u_ref, l1, l2, p1, p2, k1, k2, b1, b2, s1_ref, s2_ref, out_ref, z_ref, z2_ref, m_ref
):
    span = u_ref.shape[1]
    edge1 = jnp.zeros((rows + 4, 8, z_ref.shape[2]), F32)
    edge2 = jnp.zeros((rows + 2, 8, z_ref.shape[2]), F32)
    z_ref[:, 0:8, :] = edge1
    z_ref[:, span + 8 : span + 16, :] = edge1
    z2_ref[:, 0:8, :] = edge2
    z2_ref[:, span + 8 : span + 16, :] = edge2

    @pl.loop(0, rows + 4)
    def _(r):
        z_ref[r, 8 : span + 8, :] = dot_split(u_ref[r], l1[...])

    size = 256
    pieces = span // size

    def conv(ref, taps, bias, r, base):
        acc = jnp.broadcast_to(bias[...], (size, taps.shape[1]))
        for i in range(3):
            for j in range(3):
                acc = acc + taps[3 * i + j : 3 * i + j + 1, :] * ref[r + i, pl.ds(base + 8 * j, size), :]
        return jnp.tanh(acc)

    @pl.loop(0, (rows + 2) * pieces)
    def _(n):
        r, q = n // pieces, n % pieces
        base = pl.multiple_of(q * size, size)
        keep = mask_ref[r]
        act = conv(z_ref, k1, b1, r, base)
        s1_ref[r, pl.ds(q * (size // 32), size // 32)] = regroup((1.0 - act * act) * keep)
        mid = (u_ref[r + 1, pl.ds(base, size), :] + dot_split(act, p1[...], True)) * keep
        m_ref[r, pl.ds(base, size), :] = mid
        z2_ref[r, pl.ds(base + 8, size), :] = dot_split(mid, l2[...])

    @pl.loop(0, rows * pieces)
    def _(n):
        r, q = n // pieces, n % pieces
        base = pl.multiple_of(q * size, size)
        act = conv(z2_ref, k2, b2, r, base)
        s2_ref[r, pl.ds(q * (size // 32), size // 32)] = regroup(1.0 - act * act)
        out_ref[r, pl.ds(base, size), :] = m_ref[r + 1, pl.ds(base, size), :] + dot_split(act, p2[...], True)


def tangent_kernel(
    rows, segs, low_ref, own_ref, high_ref, turned_ref, s1_ref, s2_ref, p1, p2, kern1, kern2, lift1, lift2,
    sel_ref, rep_ref, spread_ref, maps_ref, x_ref, v_ref, t_ref, k1_ref, k2_ref, pd1, pd2,
):
    span = turned_ref.shape[2]
    tiles = span // 64
    nm = own_ref.shape[2]
    x_ref[0:2] = low_ref[...]
    x_ref[2 : rows + 2] = own_ref[...]
    x_ref[rows + 2 : rows + 4] = high_ref[...]
    v_ref[:, 0:8, :] = jnp.zeros((rows + 2, 8, segs * nm), F32)
    v_ref[:, span + 8 : span + 32, :] = jnp.zeros((rows + 2, 24, segs * nm), F32)
    column = lax.broadcasted_iota(jnp.int32, (8, 256), 1) // 64
    for kern, lift, proj, k_ref, pd in ((kern1, lift1, p1, k1_ref, pd1), (kern2, lift2, p2, k2_ref, pd2)):
        wide = dot_turned(lift[...].astype(F32), rep_ref[...], 0, HI)
        across = dot(proj[...], spread_ref[...])
        for col in range(4):
            pd[8 * col : 8 * col + 8, :] = jnp.where(column == col, across, 0.0)
        for col in range(8):
            taps = dot_turned(kern[...], sel_ref[col], 0, HI)
            k_ref[col // 4, (col % 4) * 64 : (col % 4 + 1) * 64, :] = (taps * wide).astype(BF16)
    maps_ref[...] = jnp.zeros_like(maps_ref)

    def band(slopes, pd, k_ref, h):
        scale = pd[...]
        lhs = jnp.concatenate([(slopes[s : s + 1, :] * scale).astype(BF16) for s in range(segs)], axis=0)
        return dot(lhs, k_ref[h]).astype(BF16)

    @pl.loop(0, (rows + 2) * tiles, unroll=2)
    def _(n):
        r, t = n // tiles, n % tiles
        at = pl.multiple_of(t * 64, 64)
        middle = x_ref[r + 1, pl.ds(at, 80), :]
        near = jnp.concatenate([x_ref[r, pl.ds(at, 80), :], middle, x_ref[r + 2, pl.ds(at, 96), :]], axis=0)
        middle = middle.astype(F32)
        for h in range(2):
            out = dot(band(s1_ref[r, 2 * t + h], pd1, k1_ref, h), near)
            own = middle[8 + 32 * h : 40 + 32 * h]
            for s in range(segs):
                v_ref[r, pl.ds(at + (8 + 32 * h), 32), s * nm : (s + 1) * nm] = own + out[s * 32 : (s + 1) * 32]

    @pl.loop(0, rows)
    def _(r):
        @pl.loop(0, tiles, unroll=2)
        def _(t):
            at = pl.multiple_of(t * 64, 64)
            bands = [band(s2_ref[r, 2 * t + h], pd2, k2_ref, h) for h in range(2)]
            for s in range(segs):
                lanes = slice(s * nm, (s + 1) * nm)
                middle = v_ref[r + 1, pl.ds(at, 80), lanes].astype(BF16)
                near = jnp.concatenate(
                    [
                        v_ref[r, pl.ds(at, 80), lanes].astype(BF16),
                        middle,
                        v_ref[r + 2, pl.ds(at, 96), lanes].astype(BF16),
                    ],
                    axis=0,
                )
                both = jnp.concatenate([b[s * 32 : (s + 1) * 32] for b in bands], axis=0)
                out = dot(both, near) + middle.astype(F32)[8:72]
                t_ref[pl.ds(at, 64), lanes] = out.astype(BF16)

        part = dot(turned_ref[r], t_ref[...])
        for s in range(segs):
            maps_ref[s * nm : (s + 1) * nm, :] += part[:, s * nm : (s + 1) * nm]


def close_kernel(
    segs, count, turns, mats_ref, vecs_ref, coeffs_ref, land_ref, sum_ref, all_ref, vland_ref, end_ref, start_ref,
    send_m, recv_m, send_v, recv_v, send_a, recv_a, send_s, recv_s,
):
    nm = mats_ref.shape[1]
    chunk = mats_ref.shape[0] // count
    me, turn = lax.axis_index("space"), lax.axis_index("seg")
    later, sooner = (turn + 1) % turns, (turn + turns - 1) % turns

    def share(who):
        return pl.ds(pl.multiple_of(who * chunk, 8), chunk)

    barrier = pltpu.get_barrier_semaphore()
    for d in range(1, count):
        pl.semaphore_signal(barrier, inc=1, device_id={"space": (me + d) % count}, device_id_type=MESH)
    if turns > 1:
        pl.semaphore_signal(barrier, inc=1, device_id={"seg": sooner}, device_id_type=MESH)
    pl.semaphore_wait(barrier, count - 1 + (turns > 1))

    maps, vectors = [], []
    for d in range(1, count):
        target = (me + d) % count
        copy = pltpu.make_async_remote_copy(
            src_ref=mats_ref.at[share(target)], dst_ref=land_ref.at[d],
            send_sem=send_m.at[d], recv_sem=recv_m.at[d],
            device_id={"space": target}, device_id_type=MESH,
        )
        copy.start()
        maps.append(copy)
    for d in range(1, count):
        target = (me + d) % count
        copy = pltpu.make_async_remote_copy(
            src_ref=vecs_ref, dst_ref=vland_ref.at[d],
            send_sem=send_v.at[d], recv_sem=recv_v.at[d],
            device_id={"space": target}, device_id_type=MESH,
        )
        copy.start()
        vectors.append(copy)
    total = mats_ref[share(me), :]
    for d in range(1, count):
        maps[d - 1].wait_recv()
        total = total + land_ref[d]
    sum_ref[...] = total
    gathers = []
    for d in range(1, count):
        copy = pltpu.make_async_remote_copy(
            src_ref=sum_ref, dst_ref=all_ref.at[share(me)],
            send_sem=send_a.at[d], recv_sem=recv_a.at[d],
            device_id={"space": (me + d) % count}, device_id_type=MESH,
        )
        copy.start()
        gathers.append(copy)
    all_ref[share(me), :] = total
    vland_ref[0] = vecs_ref[...]
    for copy in vectors:
        copy.wait_recv()
    vecs = jnp.zeros((segs, nm), F32)
    for who in range(count):
        vecs = vecs + vland_ref[(me + count - who) % count]
    for d in range(1, count):
        source = (me + count - d) % count
        pltpu.make_async_remote_copy(
            src_ref=sum_ref, dst_ref=all_ref.at[share(source)],
            send_sem=send_a.at[d], recv_sem=recv_a.at[d],
            device_id={"space": (me + d) % count}, device_id_type=MESH,
        ).wait_recv()

    def chain(current, keep):
        for s in range(segs):
            if keep:
                coeffs_ref[s : s + 1, :] = current[0:1, :]
            if not keep or s < segs - 1:
                current = dot_turned(current, all_ref[s * nm : (s + 1) * nm, :], 1, HI) + vecs[s : s + 1, :]
        return current

    current = jnp.zeros((8, nm), F32)
    for step in range(turns - 1):
        end_ref[step] = chain(current, False)
        copy = pltpu.make_async_remote_copy(
            src_ref=end_ref.at[step], dst_ref=start_ref.at[step],
            send_sem=send_s.at[step], recv_sem=recv_s.at[step],
            device_id={"seg": later}, device_id_type=MESH,
        )
        copy.start()
        copy.wait()
        current = jnp.where(turn == 0, 0.0, start_ref[step])
    chain(current, True)
    for copy in maps + vectors + gathers:
        copy.wait_send()


def selectors():
    sel = np.zeros((8, 9, 256), np.float32)
    rep = np.zeros((8, 256), np.float32)
    for i in range(3):
        for w in range(10):
            for g in range(8):
                lane = 80 * i + 8 * w + g
                rep[g, lane] = 1.0
                for col in range(8):
                    if 0 <= w - col < 3:
                        sel[col, 3 * i + w - col, lane] = 1.0
    return sel, rep, jnp.asarray(np.tile(np.eye(64, dtype=np.float32), (1, 4)), BF16)


VM = pl.BlockSpec(memory_space=pltpu.VMEM)
MESH = pl.DeviceIdType.MESH
SM = pl.BlockSpec(memory_space=pltpu.SMEM)


def on_device(
    modes, states, lift_one, kern_one, bias_one, proj_one, lift_two, kern_two, bias_two, proj_two
):
    fields, rows, cols, nmodes = modes.shape
    segs = states.shape[0]
    channels = lift_one.shape[0]
    count = lax.axis_size("space")
    down = [(i, i + 1) for i in range(count - 1)]
    up = [(i + 1, i) for i in range(count - 1)]

    before = lax.ppermute(states[:, :, rows - 2 :], "space", down)
    after = lax.ppermute(states[:, :, :2], "space", up)
    turns = lax.axis_size("seg")
    follow = lax.ppermute(states[0], "seg", [(i + 1, i) for i in range(turns - 1)])

    own = jnp.transpose(modes, (1, 2, 0, 3)).reshape(rows, cols * fields, nmodes)
    turned = jnp.transpose(own, (0, 2, 1))
    own = jnp.pad(own, ((0, 0), (8, 24), (0, 0)))
    low = lax.ppermute(own[rows - 2 :], "space", down)
    high = lax.ppermute(own[:2], "space", up)

    extended = jnp.concatenate([before, states, after], axis=2)
    u = jnp.transpose(extended, (2, 3, 0, 1)).reshape(rows + 4, cols * segs, fields)
    glob = lax.axis_index("space") * rows - 1 + jnp.arange(rows + 2)
    mask = ((glob >= 0) & (glob < rows * count)).astype(F32)

    groups = cols // 4
    span = cols * segs
    slope_one, slope_two, final = pl.pallas_call(
        functools.partial(advance_kernel, rows),
        out_shape=(
            jax.ShapeDtypeStruct((rows + 2, groups, segs, 4 * channels), F32),
            jax.ShapeDtypeStruct((rows, groups, segs, 4 * channels), F32),
            jax.ShapeDtypeStruct((rows, span, fields), F32),
        ),
        in_specs=[SM] + [VM] * 9,
        out_specs=(VM, VM, VM),
        scratch_shapes=[
            pltpu.VMEM((rows + 4, span + 16, channels), F32),
            pltpu.VMEM((rows + 2, span + 16, channels), F32),
            pltpu.VMEM((rows + 2, span, fields), F32),
        ],
        compiler_params=pltpu.CompilerParams(vmem_limit_bytes=56 * 2**20),
        cost_estimate=pl.CostEstimate(flops=10**8, bytes_accessed=10**7, transcendentals=10**6),
    )(
        mask, u, lift_one.T, lift_two.T, proj_one, proj_two, kern_one.T, kern_two.T,
        bias_one[None], bias_two[None],
    )
    advanced = jnp.transpose(final.reshape(rows, cols, segs, fields), (2, 3, 0, 1))
    defects = (advanced - jnp.concatenate([states[1:], follow[None]], axis=0)).astype(BF16)
    vecs = jnp.einsum("sfrw,frwk->sk", defects, modes, preferred_element_type=F32)

    sel, rep, spread = selectors()
    lines = cols * fields
    mats = pl.pallas_call(
        functools.partial(tangent_kernel, rows, segs),
        out_shape=jax.ShapeDtypeStruct((segs * nmodes, nmodes), F32),
        in_specs=[VM] * 15,
        out_specs=VM,
        scratch_shapes=[
            pltpu.VMEM((rows + 4, lines + 32, nmodes), BF16),
            pltpu.VMEM((rows + 2, lines + 32, segs * nmodes), F32),
            pltpu.VMEM((lines, segs * nmodes), BF16),
            pltpu.VMEM((2, 256, 256), BF16),
            pltpu.VMEM((2, 256, 256), BF16),
            pltpu.VMEM((32, 256), F32),
            pltpu.VMEM((32, 256), F32),
        ],
        compiler_params=pltpu.CompilerParams(vmem_limit_bytes=56 * 2**20),
        cost_estimate=pl.CostEstimate(flops=2 * 10**10, bytes_accessed=10**7, transcendentals=0),
    )(
        low, own, high, turned, slope_one, slope_two, proj_one, proj_two, kern_one.T, kern_two.T,
        lift_one.T, lift_two.T, sel, rep, spread,
    )

    chunk = segs * nmodes // count
    dma = pltpu.SemaphoreType.DMA
    coeffs = pl.pallas_call(
        functools.partial(close_kernel, segs, count, turns),
        out_shape=jax.ShapeDtypeStruct((segs, nmodes), F32),
        in_specs=[VM] * 2,
        out_specs=VM,
        scratch_shapes=[
            pltpu.VMEM((count, chunk, nmodes), F32),
            pltpu.VMEM((chunk, nmodes), F32),
            pltpu.VMEM((segs * nmodes, nmodes), F32),
            pltpu.VMEM((count, segs, nmodes), F32),
            pltpu.VMEM((turns, 8, nmodes), F32),
            pltpu.VMEM((turns, 8, nmodes), F32),
            dma((count,)), dma((count,)), dma((count,)), dma((count,)), dma((count,)), dma((count,)),
            dma((turns,)), dma((turns,)),
        ],
        compiler_params=pltpu.CompilerParams(collective_id=0, has_side_effects=True),
    )(mats, vecs)
    return advanced, coeffs


def solution(mesh):
    placed = (
        P(None, "space", None, None),
        P(("groups", "seg"), None, "space", None),
        P(), P(), P(), P(), P(), P(), P(), P(),
    )
    return jax.shard_map(
        on_device,
        mesh=mesh,
        in_specs=placed,
        out_specs=(P(("groups", "seg"), None, "space", None), P(("groups", "seg"), None)),
        check_vma=False,
    )
```

```python
import functools

import jax
import jax.numpy as jnp
import numpy as np
from jax import lax
from jax.experimental import pallas as pl
from jax.experimental.pallas import tpu as pltpu
from jax.sharding import PartitionSpec as P

HI = lax.Precision.HIGHEST
F32 = jnp.float32
BF16 = jnp.bfloat16


def dot(a, b):
    return jnp.dot(a, b, preferred_element_type=F32)


def dot_turned(a, b, side, precision=None):
    return lax.dot_general(
        a, b, (((side,), (side,)), ((), ())), precision=precision, preferred_element_type=F32
    )


def dot_split(x, weight, turned=False):
    high = x.astype(BF16)
    low = (x - high.astype(F32)).astype(BF16)
    if turned:
        return dot_turned(high, weight, 1) + dot_turned(low, weight, 1)
    return dot(high, weight) + dot(low, weight)


def regroup(x):
    x = x.reshape(x.shape[0] // 32, 4, 8, x.shape[1])
    return jnp.concatenate([x[:, a] for a in range(4)], axis=-1)


def advance_kernel(
    rows, mask_ref, u_ref, l1, l2, p1, p2, k1, k2, b1, b2, s1_ref, s2_ref, out_ref, z_ref, z2_ref, m_ref
):
    span = u_ref.shape[1]
    edge1 = jnp.zeros((rows + 4, 8, z_ref.shape[2]), F32)
    edge2 = jnp.zeros((rows + 2, 8, z_ref.shape[2]), F32)
    z_ref[:, 0:8, :] = edge1
    z_ref[:, span + 8 : span + 16, :] = edge1
    z2_ref[:, 0:8, :] = edge2
    z2_ref[:, span + 8 : span + 16, :] = edge2

    @pl.loop(0, rows + 4, unroll=2)
    def _(r):
        z_ref[r, 8 : span + 8, :] = dot_split(u_ref[r], l1[...])

    size = 256
    pieces = span // size

    def conv(ref, taps, bias, r, base):
        acc = jnp.broadcast_to(bias[...], (size, taps.shape[1]))
        for i in range(3):
            for j in range(3):
                acc = acc + taps[3 * i + j : 3 * i + j + 1, :] * ref[r + i, pl.ds(base + 8 * j, size), :]
        return jnp.tanh(acc)

    @pl.loop(0, (rows + 2) * pieces, unroll=2)
    def _(n):
        r, q = n // pieces, n % pieces
        base = pl.multiple_of(q * size, size)
        keep = mask_ref[r]
        act = conv(z_ref, k1, b1, r, base)
        s1_ref[r, pl.ds(q * (size // 32), size // 32)] = regroup((1.0 - act * act) * keep)
        mid = (u_ref[r + 1, pl.ds(base, size), :] + dot_split(act, p1[...], True)) * keep
        m_ref[r, pl.ds(base, size), :] = mid
        z2_ref[r, pl.ds(base + 8, size), :] = dot_split(mid, l2[...])

    @pl.loop(0, rows * pieces, unroll=2)
    def _(n):
        r, q = n // pieces, n % pieces
        base = pl.multiple_of(q * size, size)
        act = conv(z2_ref, k2, b2, r, base)
        s2_ref[r, pl.ds(q * (size // 32), size // 32)] = regroup(1.0 - act * act)
        out_ref[r, pl.ds(base, size), :] = m_ref[r + 1, pl.ds(base, size), :] + dot_split(act, p2[...], True)


def tangent_kernel(
    rows, segs, low_ref, own_ref, high_ref, turned_ref, s1_ref, s2_ref, p1, p2, kern1, kern2, lift1, lift2,
    sel_ref, rep_ref, spread_ref, maps_ref, x_ref, v_ref, t_ref, k1_ref, k2_ref, pd1, pd2,
):
    span = turned_ref.shape[2]
    tiles = span // 64
    nm = own_ref.shape[2]
    x_ref[0:2] = low_ref[...]
    x_ref[2 : rows + 2] = own_ref[...]
    x_ref[rows + 2 : rows + 4] = high_ref[...]
    v_ref[:, 0:8, :] = jnp.zeros((rows + 2, 8, segs * nm), F32)
    v_ref[:, span + 8 : span + 32, :] = jnp.zeros((rows + 2, 24, segs * nm), F32)
    column = lax.broadcasted_iota(jnp.int32, (8, 256), 1) // 64
    for kern, lift, proj, k_ref, pd in ((kern1, lift1, p1, k1_ref, pd1), (kern2, lift2, p2, k2_ref, pd2)):
        wide = dot_turned(lift[...].astype(F32), rep_ref[...], 0, HI)
        across = dot(proj[...], spread_ref[...])
        for col in range(4):
            pd[8 * col : 8 * col + 8, :] = jnp.where(column == col, across, 0.0)
        for col in range(8):
            taps = dot_turned(kern[...], sel_ref[col], 0, HI)
            k_ref[col // 4, (col % 4) * 64 : (col % 4 + 1) * 64, :] = (taps * wide).astype(BF16)
    maps_ref[...] = jnp.zeros_like(maps_ref)

    def band(slopes, pd, k_ref, h):
        scale = pd[...]
        lhs = jnp.concatenate([(slopes[s : s + 1, :] * scale).astype(BF16) for s in range(segs)], axis=0)
        return dot(lhs, k_ref[h]).astype(BF16)

    @pl.loop(0, (rows + 2) * tiles, unroll=4)
    def _(n):
        r, t = n // tiles, n % tiles
        at = pl.multiple_of(t * 64, 64)
        middle = x_ref[r + 1, pl.ds(at, 80), :]
        near = jnp.concatenate([x_ref[r, pl.ds(at, 80), :], middle, x_ref[r + 2, pl.ds(at, 96), :]], axis=0)
        middle = middle.astype(F32)
        for h in range(2):
            out = dot(band(s1_ref[r, 2 * t + h], pd1, k1_ref, h), near)
            own = middle[8 + 32 * h : 40 + 32 * h]
            for s in range(segs):
                v_ref[r, pl.ds(at + (8 + 32 * h), 32), s * nm : (s + 1) * nm] = own + out[s * 32 : (s + 1) * 32]

    @pl.loop(0, rows)
    def _(r):
        @pl.loop(0, tiles, unroll=4)
        def _(t):
            at = pl.multiple_of(t * 64, 64)
            bands = [band(s2_ref[r, 2 * t + h], pd2, k2_ref, h) for h in range(2)]
            for s in range(segs):
                lanes = slice(s * nm, (s + 1) * nm)
                middle = v_ref[r + 1, pl.ds(at, 80), lanes].astype(BF16)
                near = jnp.concatenate(
                    [
                        v_ref[r, pl.ds(at, 80), lanes].astype(BF16),
                        middle,
                        v_ref[r + 2, pl.ds(at, 96), lanes].astype(BF16),
                    ],
                    axis=0,
                )
                both = jnp.concatenate([b[s * 32 : (s + 1) * 32] for b in bands], axis=0)
                out = dot(both, near) + middle.astype(F32)[8:72]
                t_ref[pl.ds(at, 64), lanes] = out.astype(BF16)

        part = dot(turned_ref[r], t_ref[...])
        for s in range(segs):
            maps_ref[s * nm : (s + 1) * nm, :] += part[:, s * nm : (s + 1) * nm]


def close_kernel(
    segs, count, turns, mats_ref, vecs_ref, coeffs_ref, land_ref, sum_ref, all_ref, vland_ref, end_ref, start_ref,
    send_m, recv_m, send_v, recv_v, send_a, recv_a, send_s, recv_s,
):
    nm = mats_ref.shape[1]
    chunk = mats_ref.shape[0] // count
    me, turn = lax.axis_index("space"), lax.axis_index("seg")
    later, sooner = (turn + 1) % turns, (turn + turns - 1) % turns

    def share(who):
        return pl.ds(pl.multiple_of(who * chunk, 8), chunk)

    barrier = pltpu.get_barrier_semaphore()
    for d in range(1, count):
        pl.semaphore_signal(barrier, inc=1, device_id={"space": (me + d) % count}, device_id_type=MESH)
    if turns > 1:
        pl.semaphore_signal(barrier, inc=1, device_id={"seg": sooner}, device_id_type=MESH)
    pl.semaphore_wait(barrier, count - 1 + (turns > 1))

    maps, vectors = [], []
    for d in range(1, count):
        target = (me + d) % count
        copy = pltpu.make_async_remote_copy(
            src_ref=mats_ref.at[share(target)], dst_ref=land_ref.at[d],
            send_sem=send_m.at[d], recv_sem=recv_m.at[d],
            device_id={"space": target}, device_id_type=MESH,
        )
        copy.start()
        maps.append(copy)
    for d in range(1, count):
        target = (me + d) % count
        copy = pltpu.make_async_remote_copy(
            src_ref=vecs_ref, dst_ref=vland_ref.at[d],
            send_sem=send_v.at[d], recv_sem=recv_v.at[d],
            device_id={"space": target}, device_id_type=MESH,
        )
        copy.start()
        vectors.append(copy)
    total = mats_ref[share(me), :]
    for d in range(1, count):
        maps[d - 1].wait_recv()
        total = total + land_ref[d]
    sum_ref[...] = total
    gathers = []
    for d in range(1, count):
        copy = pltpu.make_async_remote_copy(
            src_ref=sum_ref, dst_ref=all_ref.at[share(me)],
            send_sem=send_a.at[d], recv_sem=recv_a.at[d],
            device_id={"space": (me + d) % count}, device_id_type=MESH,
        )
        copy.start()
        gathers.append(copy)
    all_ref[share(me), :] = total
    vland_ref[0] = vecs_ref[...]
    for copy in vectors:
        copy.wait_recv()
    vecs = jnp.zeros((segs, nm), F32)
    for who in range(count):
        vecs = vecs + vland_ref[(me + count - who) % count]
    for d in range(1, count):
        source = (me + count - d) % count
        pltpu.make_async_remote_copy(
            src_ref=sum_ref, dst_ref=all_ref.at[share(source)],
            send_sem=send_a.at[d], recv_sem=recv_a.at[d],
            device_id={"space": (me + d) % count}, device_id_type=MESH,
        ).wait_recv()

    def chain(current, keep):
        for s in range(segs):
            if keep:
                coeffs_ref[s : s + 1, :] = current[0:1, :]
            if not keep or s < segs - 1:
                current = dot_turned(current, all_ref[s * nm : (s + 1) * nm, :], 1, HI) + vecs[s : s + 1, :]
        return current

    current = jnp.zeros((8, nm), F32)
    for step in range(turns - 1):
        end_ref[step] = chain(current, False)
        copy = pltpu.make_async_remote_copy(
            src_ref=end_ref.at[step], dst_ref=start_ref.at[step],
            send_sem=send_s.at[step], recv_sem=recv_s.at[step],
            device_id={"seg": later}, device_id_type=MESH,
        )
        copy.start()
        copy.wait()
        current = jnp.where(turn == 0, 0.0, start_ref[step])
    chain(current, True)
    for copy in maps + vectors + gathers:
        copy.wait_send()


def selectors():
    sel = np.zeros((8, 9, 256), np.float32)
    rep = np.zeros((8, 256), np.float32)
    for i in range(3):
        for w in range(10):
            for g in range(8):
                lane = 80 * i + 8 * w + g
                rep[g, lane] = 1.0
                for col in range(8):
                    if 0 <= w - col < 3:
                        sel[col, 3 * i + w - col, lane] = 1.0
    return sel, rep, jnp.asarray(np.tile(np.eye(64, dtype=np.float32), (1, 4)), BF16)


VM = pl.BlockSpec(memory_space=pltpu.VMEM)
MESH = pl.DeviceIdType.MESH
SM = pl.BlockSpec(memory_space=pltpu.SMEM)


def on_device(
    modes, states, lift_one, kern_one, bias_one, proj_one, lift_two, kern_two, bias_two, proj_two
):
    fields, rows, cols, nmodes = modes.shape
    segs = states.shape[0]
    channels = lift_one.shape[0]
    count = lax.axis_size("space")
    down = [(i, i + 1) for i in range(count - 1)]
    up = [(i + 1, i) for i in range(count - 1)]

    before = lax.ppermute(states[:, :, rows - 2 :], "space", down)
    after = lax.ppermute(states[:, :, :2], "space", up)
    turns = lax.axis_size("seg")
    follow = lax.ppermute(states[0], "seg", [(i + 1, i) for i in range(turns - 1)])

    own = jnp.transpose(modes, (1, 2, 0, 3)).reshape(rows, cols * fields, nmodes)
    turned = jnp.transpose(own, (0, 2, 1))
    own = jnp.pad(own, ((0, 0), (8, 24), (0, 0)))
    low = lax.ppermute(own[rows - 2 :], "space", down)
    high = lax.ppermute(own[:2], "space", up)

    extended = jnp.concatenate([before, states, after], axis=2)
    u = jnp.transpose(extended, (2, 3, 0, 1)).reshape(rows + 4, cols * segs, fields)
    glob = lax.axis_index("space") * rows - 1 + jnp.arange(rows + 2)
    mask = ((glob >= 0) & (glob < rows * count)).astype(F32)

    groups = cols // 4
    span = cols * segs
    slope_one, slope_two, final = pl.pallas_call(
        functools.partial(advance_kernel, rows),
        out_shape=(
            jax.ShapeDtypeStruct((rows + 2, groups, segs, 4 * channels), F32),
            jax.ShapeDtypeStruct((rows, groups, segs, 4 * channels), F32),
            jax.ShapeDtypeStruct((rows, span, fields), F32),
        ),
        in_specs=[SM] + [VM] * 9,
        out_specs=(VM, VM, VM),
        scratch_shapes=[
            pltpu.VMEM((rows + 4, span + 16, channels), F32),
            pltpu.VMEM((rows + 2, span + 16, channels), F32),
            pltpu.VMEM((rows + 2, span, fields), F32),
        ],
        compiler_params=pltpu.CompilerParams(vmem_limit_bytes=56 * 2**20),
        cost_estimate=pl.CostEstimate(flops=10**8, bytes_accessed=10**7, transcendentals=10**6),
    )(
        mask, u, lift_one.T, lift_two.T, proj_one, proj_two, kern_one.T, kern_two.T,
        bias_one[None], bias_two[None],
    )
    advanced = jnp.transpose(final.reshape(rows, cols, segs, fields), (2, 3, 0, 1))
    defects = (advanced - jnp.concatenate([states[1:], follow[None]], axis=0)).astype(BF16)
    vecs = jnp.einsum("sfrw,frwk->sk", defects, modes, preferred_element_type=F32)

    sel, rep, spread = selectors()
    lines = cols * fields
    mats = pl.pallas_call(
        functools.partial(tangent_kernel, rows, segs),
        out_shape=jax.ShapeDtypeStruct((segs * nmodes, nmodes), F32),
        in_specs=[VM] * 15,
        out_specs=VM,
        scratch_shapes=[
            pltpu.VMEM((rows + 4, lines + 32, nmodes), BF16),
            pltpu.VMEM((rows + 2, lines + 32, segs * nmodes), F32),
            pltpu.VMEM((lines, segs * nmodes), BF16),
            pltpu.VMEM((2, 256, 256), BF16),
            pltpu.VMEM((2, 256, 256), BF16),
            pltpu.VMEM((32, 256), F32),
            pltpu.VMEM((32, 256), F32),
        ],
        compiler_params=pltpu.CompilerParams(vmem_limit_bytes=56 * 2**20),
        cost_estimate=pl.CostEstimate(flops=2 * 10**10, bytes_accessed=10**7, transcendentals=0),
    )(
        low, own, high, turned, slope_one, slope_two, proj_one, proj_two, kern_one.T, kern_two.T,
        lift_one.T, lift_two.T, sel, rep, spread,
    )

    chunk = segs * nmodes // count
    dma = pltpu.SemaphoreType.DMA
    coeffs = pl.pallas_call(
        functools.partial(close_kernel, segs, count, turns),
        out_shape=jax.ShapeDtypeStruct((segs, nmodes), F32),
        in_specs=[VM] * 2,
        out_specs=VM,
        scratch_shapes=[
            pltpu.VMEM((count, chunk, nmodes), F32),
            pltpu.VMEM((chunk, nmodes), F32),
            pltpu.VMEM((segs * nmodes, nmodes), F32),
            pltpu.VMEM((count, segs, nmodes), F32),
            pltpu.VMEM((turns, 8, nmodes), F32),
            pltpu.VMEM((turns, 8, nmodes), F32),
            dma((count,)), dma((count,)), dma((count,)), dma((count,)), dma((count,)), dma((count,)),
            dma((turns,)), dma((turns,)),
        ],
        compiler_params=pltpu.CompilerParams(collective_id=0, has_side_effects=True),
    )(mats, vecs)
    return advanced, coeffs


def solution(mesh):
    placed = (
        P(None, "space", None, None),
        P(("groups", "seg"), None, "space", None),
        P(), P(), P(), P(), P(), P(), P(), P(),
    )
    return jax.shard_map(
        on_device,
        mesh=mesh,
        in_specs=placed,
        out_specs=(P(("groups", "seg"), None, "space", None), P(("groups", "seg"), None)),
        check_vma=False,
    )
```

```python
import functools

import jax
import jax.numpy as jnp
import numpy as np
from jax import lax
from jax.experimental import pallas as pl
from jax.experimental.pallas import tpu as pltpu
from jax.sharding import PartitionSpec as P

HI = lax.Precision.HIGHEST
F32 = jnp.float32
BF16 = jnp.bfloat16


def dot(a, b):
    return jnp.dot(a, b, preferred_element_type=F32)


def dot_turned(a, b, side, precision=None):
    return lax.dot_general(
        a, b, (((side,), (side,)), ((), ())), precision=precision, preferred_element_type=F32
    )


def dot_split(x, weight, turned=False):
    high = x.astype(BF16)
    low = (x - high.astype(F32)).astype(BF16)
    if turned:
        return dot_turned(high, weight, 1) + dot_turned(low, weight, 1)
    return dot(high, weight) + dot(low, weight)


def regroup(x):
    x = x.reshape(x.shape[0] // 32, 4, 8, x.shape[1])
    return jnp.concatenate([x[:, a] for a in range(4)], axis=-1)


def advance_kernel(
    rows, mask_ref, u_ref, l1, l2, p1, p2, k1, k2, b1, b2, s1_ref, s2_ref, out_ref, z_ref, z2_ref, m_ref
):
    span = u_ref.shape[1]
    edge1 = jnp.zeros((rows + 4, 8, z_ref.shape[2]), F32)
    edge2 = jnp.zeros((rows + 2, 8, z_ref.shape[2]), F32)
    z_ref[:, 0:8, :] = edge1
    z_ref[:, span + 8 : span + 16, :] = edge1
    z2_ref[:, 0:8, :] = edge2
    z2_ref[:, span + 8 : span + 16, :] = edge2

    @pl.loop(0, rows + 4, unroll=4)
    def _(r):
        z_ref[r, 8 : span + 8, :] = dot_split(u_ref[r], l1[...])

    size = 256
    pieces = span // size

    def conv(ref, taps, bias, r, base):
        acc = jnp.broadcast_to(bias[...], (size, taps.shape[1]))
        for i in range(3):
            for j in range(3):
                acc = acc + taps[3 * i + j : 3 * i + j + 1, :] * ref[r + i, pl.ds(base + 8 * j, size), :]
        return jnp.tanh(acc)

    @pl.loop(0, (rows + 2) * pieces, unroll=4)
    def _(n):
        r, q = n // pieces, n % pieces
        base = pl.multiple_of(q * size, size)
        keep = mask_ref[r]
        act = conv(z_ref, k1, b1, r, base)
        s1_ref[r, pl.ds(q * (size // 32), size // 32)] = regroup((1.0 - act * act) * keep)
        mid = (u_ref[r + 1, pl.ds(base, size), :] + dot_split(act, p1[...], True)) * keep
        m_ref[r, pl.ds(base, size), :] = mid
        z2_ref[r, pl.ds(base + 8, size), :] = dot_split(mid, l2[...])

    @pl.loop(0, rows * pieces, unroll=4)
    def _(n):
        r, q = n // pieces, n % pieces
        base = pl.multiple_of(q * size, size)
        act = conv(z2_ref, k2, b2, r, base)
        s2_ref[r, pl.ds(q * (size // 32), size // 32)] = regroup(1.0 - act * act)
        out_ref[r, pl.ds(base, size), :] = m_ref[r + 1, pl.ds(base, size), :] + dot_split(act, p2[...], True)


def tangent_kernel(
    rows, segs, low_ref, own_ref, high_ref, turned_ref, s1_ref, s2_ref, p1, p2, kern1, kern2, lift1, lift2,
    sel_ref, rep_ref, spread_ref, maps_ref, x_ref, v_ref, t_ref, k1_ref, k2_ref, pd1, pd2,
):
    span = turned_ref.shape[2]
    tiles = span // 64
    nm = own_ref.shape[2]
    x_ref[0:2] = low_ref[...]
    x_ref[2 : rows + 2] = own_ref[...]
    x_ref[rows + 2 : rows + 4] = high_ref[...]
    v_ref[:, 0:8, :] = jnp.zeros((rows + 2, 8, segs * nm), F32)
    v_ref[:, span + 8 : span + 32, :] = jnp.zeros((rows + 2, 24, segs * nm), F32)
    column = lax.broadcasted_iota(jnp.int32, (8, 256), 1) // 64
    for kern, lift, proj, k_ref, pd in ((kern1, lift1, p1, k1_ref, pd1), (kern2, lift2, p2, k2_ref, pd2)):
        wide = dot_turned(lift[...].astype(F32), rep_ref[...], 0, HI)
        across = dot(proj[...], spread_ref[...])
        for col in range(4):
            pd[8 * col : 8 * col + 8, :] = jnp.where(column == col, across, 0.0)
        for col in range(8):
            taps = dot_turned(kern[...], sel_ref[col], 0, HI)
            k_ref[col // 4, (col % 4) * 64 : (col % 4 + 1) * 64, :] = (taps * wide).astype(BF16)
    maps_ref[...] = jnp.zeros_like(maps_ref)

    def band(slopes, pd, k_ref, h):
        scale = pd[...]
        lhs = jnp.concatenate([(slopes[s : s + 1, :] * scale).astype(BF16) for s in range(segs)], axis=0)
        return dot(lhs, k_ref[h]).astype(BF16)

    @pl.loop(0, (rows + 2) * tiles, unroll=8)
    def _(n):
        r, t = n // tiles, n % tiles
        at = pl.multiple_of(t * 64, 64)
        middle = x_ref[r + 1, pl.ds(at, 80), :]
        near = jnp.concatenate([x_ref[r, pl.ds(at, 80), :], middle, x_ref[r + 2, pl.ds(at, 96), :]], axis=0)
        middle = middle.astype(F32)
        for h in range(2):
            out = dot(band(s1_ref[r, 2 * t + h], pd1, k1_ref, h), near)
            own = middle[8 + 32 * h : 40 + 32 * h]
            for s in range(segs):
                v_ref[r, pl.ds(at + (8 + 32 * h), 32), s * nm : (s + 1) * nm] = own + out[s * 32 : (s + 1) * 32]

    @pl.loop(0, rows)
    def _(r):
        @pl.loop(0, tiles, unroll=8)
        def _(t):
            at = pl.multiple_of(t * 64, 64)
            bands = [band(s2_ref[r, 2 * t + h], pd2, k2_ref, h) for h in range(2)]
            for s in range(segs):
                lanes = slice(s * nm, (s + 1) * nm)
                middle = v_ref[r + 1, pl.ds(at, 80), lanes].astype(BF16)
                near = jnp.concatenate(
                    [
                        v_ref[r, pl.ds(at, 80), lanes].astype(BF16),
                        middle,
                        v_ref[r + 2, pl.ds(at, 96), lanes].astype(BF16),
                    ],
                    axis=0,
                )
                both = jnp.concatenate([b[s * 32 : (s + 1) * 32] for b in bands], axis=0)
                out = dot(both, near) + middle.astype(F32)[8:72]
                t_ref[pl.ds(at, 64), lanes] = out.astype(BF16)

        part = dot(turned_ref[r], t_ref[...])
        for s in range(segs):
            maps_ref[s * nm : (s + 1) * nm, :] += part[:, s * nm : (s + 1) * nm]


def close_kernel(
    segs, count, turns, mats_ref, vecs_ref, coeffs_ref, land_ref, sum_ref, all_ref, vland_ref, end_ref, start_ref,
    send_m, recv_m, send_v, recv_v, send_a, recv_a, send_s, recv_s,
):
    nm = mats_ref.shape[1]
    chunk = mats_ref.shape[0] // count
    me, turn = lax.axis_index("space"), lax.axis_index("seg")
    later, sooner = (turn + 1) % turns, (turn + turns - 1) % turns

    def share(who):
        return pl.ds(pl.multiple_of(who * chunk, 8), chunk)

    barrier = pltpu.get_barrier_semaphore()
    for d in range(1, count):
        pl.semaphore_signal(barrier, inc=1, device_id={"space": (me + d) % count}, device_id_type=MESH)
    if turns > 1:
        pl.semaphore_signal(barrier, inc=1, device_id={"seg": sooner}, device_id_type=MESH)
    pl.semaphore_wait(barrier, count - 1 + (turns > 1))

    maps, vectors = [], []
    for d in range(1, count):
        target = (me + d) % count
        copy = pltpu.make_async_remote_copy(
            src_ref=mats_ref.at[share(target)], dst_ref=land_ref.at[d],
            send_sem=send_m.at[d], recv_sem=recv_m.at[d],
            device_id={"space": target}, device_id_type=MESH,
        )
        copy.start()
        maps.append(copy)
    for d in range(1, count):
        target = (me + d) % count
        copy = pltpu.make_async_remote_copy(
            src_ref=vecs_ref, dst_ref=vland_ref.at[d],
            send_sem=send_v.at[d], recv_sem=recv_v.at[d],
            device_id={"space": target}, device_id_type=MESH,
        )
        copy.start()
        vectors.append(copy)
    total = mats_ref[share(me), :]
    for d in range(1, count):
        maps[d - 1].wait_recv()
        total = total + land_ref[d]
    sum_ref[...] = total
    gathers = []
    for d in range(1, count):
        copy = pltpu.make_async_remote_copy(
            src_ref=sum_ref, dst_ref=all_ref.at[share(me)],
            send_sem=send_a.at[d], recv_sem=recv_a.at[d],
            device_id={"space": (me + d) % count}, device_id_type=MESH,
        )
        copy.start()
        gathers.append(copy)
    all_ref[share(me), :] = total
    vland_ref[0] = vecs_ref[...]
    for copy in vectors:
        copy.wait_recv()
    vecs = jnp.zeros((segs, nm), F32)
    for who in range(count):
        vecs = vecs + vland_ref[(me + count - who) % count]
    for d in range(1, count):
        source = (me + count - d) % count
        pltpu.make_async_remote_copy(
            src_ref=sum_ref, dst_ref=all_ref.at[share(source)],
            send_sem=send_a.at[d], recv_sem=recv_a.at[d],
            device_id={"space": (me + d) % count}, device_id_type=MESH,
        ).wait_recv()

    def chain(current, keep):
        for s in range(segs):
            if keep:
                coeffs_ref[s : s + 1, :] = current[0:1, :]
            if not keep or s < segs - 1:
                current = dot_turned(current, all_ref[s * nm : (s + 1) * nm, :], 1, HI) + vecs[s : s + 1, :]
        return current

    current = jnp.zeros((8, nm), F32)
    for step in range(turns - 1):
        end_ref[step] = chain(current, False)
        copy = pltpu.make_async_remote_copy(
            src_ref=end_ref.at[step], dst_ref=start_ref.at[step],
            send_sem=send_s.at[step], recv_sem=recv_s.at[step],
            device_id={"seg": later}, device_id_type=MESH,
        )
        copy.start()
        copy.wait()
        current = jnp.where(turn == 0, 0.0, start_ref[step])
    chain(current, True)
    for copy in maps + vectors + gathers:
        copy.wait_send()


def selectors():
    sel = np.zeros((8, 9, 256), np.float32)
    rep = np.zeros((8, 256), np.float32)
    for i in range(3):
        for w in range(10):
            for g in range(8):
                lane = 80 * i + 8 * w + g
                rep[g, lane] = 1.0
                for col in range(8):
                    if 0 <= w - col < 3:
                        sel[col, 3 * i + w - col, lane] = 1.0
    return sel, rep, jnp.asarray(np.tile(np.eye(64, dtype=np.float32), (1, 4)), BF16)


VM = pl.BlockSpec(memory_space=pltpu.VMEM)
MESH = pl.DeviceIdType.MESH
SM = pl.BlockSpec(memory_space=pltpu.SMEM)


def on_device(
    modes, states, lift_one, kern_one, bias_one, proj_one, lift_two, kern_two, bias_two, proj_two
):
    fields, rows, cols, nmodes = modes.shape
    segs = states.shape[0]
    channels = lift_one.shape[0]
    count = lax.axis_size("space")
    down = [(i, i + 1) for i in range(count - 1)]
    up = [(i + 1, i) for i in range(count - 1)]

    before = lax.ppermute(states[:, :, rows - 2 :], "space", down)
    after = lax.ppermute(states[:, :, :2], "space", up)
    turns = lax.axis_size("seg")
    follow = lax.ppermute(states[0], "seg", [(i + 1, i) for i in range(turns - 1)])

    own = jnp.transpose(modes, (1, 2, 0, 3)).reshape(rows, cols * fields, nmodes)
    turned = jnp.transpose(own, (0, 2, 1))
    own = jnp.pad(own, ((0, 0), (8, 24), (0, 0)))
    low = lax.ppermute(own[rows - 2 :], "space", down)
    high = lax.ppermute(own[:2], "space", up)

    extended = jnp.concatenate([before, states, after], axis=2)
    u = jnp.transpose(extended, (2, 3, 0, 1)).reshape(rows + 4, cols * segs, fields)
    glob = lax.axis_index("space") * rows - 1 + jnp.arange(rows + 2)
    mask = ((glob >= 0) & (glob < rows * count)).astype(F32)

    groups = cols // 4
    span = cols * segs
    slope_one, slope_two, final = pl.pallas_call(
        functools.partial(advance_kernel, rows),
        out_shape=(
            jax.ShapeDtypeStruct((rows + 2, groups, segs, 4 * channels), F32),
            jax.ShapeDtypeStruct((rows, groups, segs, 4 * channels), F32),
            jax.ShapeDtypeStruct((rows, span, fields), F32),
        ),
        in_specs=[SM] + [VM] * 9,
        out_specs=(VM, VM, VM),
        scratch_shapes=[
            pltpu.VMEM((rows + 4, span + 16, channels), F32),
            pltpu.VMEM((rows + 2, span + 16, channels), F32),
            pltpu.VMEM((rows + 2, span, fields), F32),
        ],
        compiler_params=pltpu.CompilerParams(vmem_limit_bytes=56 * 2**20),
        cost_estimate=pl.CostEstimate(flops=10**8, bytes_accessed=10**7, transcendentals=10**6),
    )(
        mask, u, lift_one.T, lift_two.T, proj_one, proj_two, kern_one.T, kern_two.T,
        bias_one[None], bias_two[None],
    )
    advanced = jnp.transpose(final.reshape(rows, cols, segs, fields), (2, 3, 0, 1))
    defects = (advanced - jnp.concatenate([states[1:], follow[None]], axis=0)).astype(BF16)
    vecs = jnp.einsum("sfrw,frwk->sk", defects, modes, preferred_element_type=F32)

    sel, rep, spread = selectors()
    lines = cols * fields
    mats = pl.pallas_call(
        functools.partial(tangent_kernel, rows, segs),
        out_shape=jax.ShapeDtypeStruct((segs * nmodes, nmodes), F32),
        in_specs=[VM] * 15,
        out_specs=VM,
        scratch_shapes=[
            pltpu.VMEM((rows + 4, lines + 32, nmodes), BF16),
            pltpu.VMEM((rows + 2, lines + 32, segs * nmodes), F32),
            pltpu.VMEM((lines, segs * nmodes), BF16),
            pltpu.VMEM((2, 256, 256), BF16),
            pltpu.VMEM((2, 256, 256), BF16),
            pltpu.VMEM((32, 256), F32),
            pltpu.VMEM((32, 256), F32),
        ],
        compiler_params=pltpu.CompilerParams(vmem_limit_bytes=56 * 2**20),
        cost_estimate=pl.CostEstimate(flops=2 * 10**10, bytes_accessed=10**7, transcendentals=0),
    )(
        low, own, high, turned, slope_one, slope_two, proj_one, proj_two, kern_one.T, kern_two.T,
        lift_one.T, lift_two.T, sel, rep, spread,
    )

    chunk = segs * nmodes // count
    dma = pltpu.SemaphoreType.DMA
    coeffs = pl.pallas_call(
        functools.partial(close_kernel, segs, count, turns),
        out_shape=jax.ShapeDtypeStruct((segs, nmodes), F32),
        in_specs=[VM] * 2,
        out_specs=VM,
        scratch_shapes=[
            pltpu.VMEM((count, chunk, nmodes), F32),
            pltpu.VMEM((chunk, nmodes), F32),
            pltpu.VMEM((segs * nmodes, nmodes), F32),
            pltpu.VMEM((count, segs, nmodes), F32),
            pltpu.VMEM((turns, 8, nmodes), F32),
            pltpu.VMEM((turns, 8, nmodes), F32),
            dma((count,)), dma((count,)), dma((count,)), dma((count,)), dma((count,)), dma((count,)),
            dma((turns,)), dma((turns,)),
        ],
        compiler_params=pltpu.CompilerParams(collective_id=0, has_side_effects=True),
    )(mats, vecs)
    return advanced, coeffs


def solution(mesh):
    placed = (
        P(None, "space", None, None),
        P(("groups", "seg"), None, "space", None),
        P(), P(), P(), P(), P(), P(), P(), P(),
    )
    return jax.shard_map(
        on_device,
        mesh=mesh,
        in_specs=placed,
        out_specs=(P(("groups", "seg"), None, "space", None), P(("groups", "seg"), None)),
        check_vma=False,
    )
```

```python
import functools

import jax
import jax.numpy as jnp
import numpy as np
from jax import lax
from jax.experimental import pallas as pl
from jax.experimental.pallas import tpu as pltpu
from jax.sharding import PartitionSpec as P

HI = lax.Precision.HIGHEST
F32 = jnp.float32
BF16 = jnp.bfloat16


def dot(a, b):
    return jnp.dot(a, b, preferred_element_type=F32)


def dot_turned(a, b, side, precision=None):
    return lax.dot_general(
        a, b, (((side,), (side,)), ((), ())), precision=precision, preferred_element_type=F32
    )


def dot_split(x, weight, turned=False):
    high = x.astype(BF16)
    low = (x - high.astype(F32)).astype(BF16)
    if turned:
        return dot_turned(high, weight, 1) + dot_turned(low, weight, 1)
    return dot(high, weight) + dot(low, weight)


def regroup(x):
    x = x.reshape(x.shape[0] // 32, 4, 8, x.shape[1])
    return jnp.concatenate([x[:, a] for a in range(4)], axis=-1)


def advance_kernel(
    rows, mask_ref, u_ref, l1, l2, p1, p2, k1, k2, b1, b2, s1_ref, s2_ref, out_ref, z_ref, z2_ref, m_ref
):
    span = u_ref.shape[1]
    edge1 = jnp.zeros((rows + 4, 8, z_ref.shape[2]), F32)
    edge2 = jnp.zeros((rows + 2, 8, z_ref.shape[2]), F32)
    z_ref[:, 0:8, :] = edge1
    z_ref[:, span + 8 : span + 16, :] = edge1
    z2_ref[:, 0:8, :] = edge2
    z2_ref[:, span + 8 : span + 16, :] = edge2

    @pl.loop(0, rows + 4, unroll=8)
    def _(r):
        z_ref[r, 8 : span + 8, :] = dot_split(u_ref[r], l1[...])

    size = 256
    pieces = span // size

    def conv(ref, taps, bias, r, base):
        acc = jnp.broadcast_to(bias[...], (size, taps.shape[1]))
        for i in range(3):
            for j in range(3):
                acc = acc + taps[3 * i + j : 3 * i + j + 1, :] * ref[r + i, pl.ds(base + 8 * j, size), :]
        return jnp.tanh(acc)

    @pl.loop(0, (rows + 2) * pieces, unroll=8)
    def _(n):
        r, q = n // pieces, n % pieces
        base = pl.multiple_of(q * size, size)
        keep = mask_ref[r]
        act = conv(z_ref, k1, b1, r, base)
        s1_ref[r, pl.ds(q * (size // 32), size // 32)] = regroup((1.0 - act * act) * keep)
        mid = (u_ref[r + 1, pl.ds(base, size), :] + dot_split(act, p1[...], True)) * keep
        m_ref[r, pl.ds(base, size), :] = mid
        z2_ref[r, pl.ds(base + 8, size), :] = dot_split(mid, l2[...])

    @pl.loop(0, rows * pieces, unroll=8)
    def _(n):
        r, q = n // pieces, n % pieces
        base = pl.multiple_of(q * size, size)
        act = conv(z2_ref, k2, b2, r, base)
        s2_ref[r, pl.ds(q * (size // 32), size // 32)] = regroup(1.0 - act * act)
        out_ref[r, pl.ds(base, size), :] = m_ref[r + 1, pl.ds(base, size), :] + dot_split(act, p2[...], True)


def tangent_kernel(
    rows, segs, low_ref, own_ref, high_ref, turned_ref, s1_ref, s2_ref, p1, p2, kern1, kern2, lift1, lift2,
    sel_ref, rep_ref, spread_ref, maps_ref, x_ref, v_ref, t_ref, k1_ref, k2_ref, pd1, pd2,
):
    span = turned_ref.shape[2]
    tiles = span // 64
    nm = own_ref.shape[2]
    x_ref[0:2] = low_ref[...]
    x_ref[2 : rows + 2] = own_ref[...]
    x_ref[rows + 2 : rows + 4] = high_ref[...]
    v_ref[:, 0:8, :] = jnp.zeros((rows + 2, 8, segs * nm), F32)
    v_ref[:, span + 8 : span + 32, :] = jnp.zeros((rows + 2, 24, segs * nm), F32)
    column = lax.broadcasted_iota(jnp.int32, (8, 256), 1) // 64
    for kern, lift, proj, k_ref, pd in ((kern1, lift1, p1, k1_ref, pd1), (kern2, lift2, p2, k2_ref, pd2)):
        wide = dot_turned(lift[...].astype(F32), rep_ref[...], 0, HI)
        across = dot(proj[...], spread_ref[...])
        for col in range(4):
            pd[8 * col : 8 * col + 8, :] = jnp.where(column == col, across, 0.0)
        for col in range(8):
            taps = dot_turned(kern[...], sel_ref[col], 0, HI)
            k_ref[col // 4, (col % 4) * 64 : (col % 4 + 1) * 64, :] = (taps * wide).astype(BF16)
    maps_ref[...] = jnp.zeros_like(maps_ref)

    def band(slopes, pd, k_ref, h):
        scale = pd[...]
        lhs = jnp.concatenate([(slopes[s : s + 1, :] * scale).astype(BF16) for s in range(segs)], axis=0)
        return dot(lhs, k_ref[h]).astype(BF16)

    @pl.loop(0, (rows + 2) * tiles, unroll=16)
    def _(n):
        r, t = n // tiles, n % tiles
        at = pl.multiple_of(t * 64, 64)
        middle = x_ref[r + 1, pl.ds(at, 80), :]
        near = jnp.concatenate([x_ref[r, pl.ds(at, 80), :], middle, x_ref[r + 2, pl.ds(at, 96), :]], axis=0)
        middle = middle.astype(F32)
        for h in range(2):
            out = dot(band(s1_ref[r, 2 * t + h], pd1, k1_ref, h), near)
            own = middle[8 + 32 * h : 40 + 32 * h]
            for s in range(segs):
                v_ref[r, pl.ds(at + (8 + 32 * h), 32), s * nm : (s + 1) * nm] = own + out[s * 32 : (s + 1) * 32]

    @pl.loop(0, rows)
    def _(r):
        @pl.loop(0, tiles, unroll=16)
        def _(t):
            at = pl.multiple_of(t * 64, 64)
            bands = [band(s2_ref[r, 2 * t + h], pd2, k2_ref, h) for h in range(2)]
            for s in range(segs):
                lanes = slice(s * nm, (s + 1) * nm)
                middle = v_ref[r + 1, pl.ds(at, 80), lanes].astype(BF16)
                near = jnp.concatenate(
                    [
                        v_ref[r, pl.ds(at, 80), lanes].astype(BF16),
                        middle,
                        v_ref[r + 2, pl.ds(at, 96), lanes].astype(BF16),
                    ],
                    axis=0,
                )
                both = jnp.concatenate([b[s * 32 : (s + 1) * 32] for b in bands], axis=0)
                out = dot(both, near) + middle.astype(F32)[8:72]
                t_ref[pl.ds(at, 64), lanes] = out.astype(BF16)

        part = dot(turned_ref[r], t_ref[...])
        for s in range(segs):
            maps_ref[s * nm : (s + 1) * nm, :] += part[:, s * nm : (s + 1) * nm]


def close_kernel(
    segs, count, turns, mats_ref, vecs_ref, coeffs_ref, land_ref, sum_ref, all_ref, vland_ref, end_ref, start_ref,
    send_m, recv_m, send_v, recv_v, send_a, recv_a, send_s, recv_s,
):
    nm = mats_ref.shape[1]
    chunk = mats_ref.shape[0] // count
    me, turn = lax.axis_index("space"), lax.axis_index("seg")
    later, sooner = (turn + 1) % turns, (turn + turns - 1) % turns

    def share(who):
        return pl.ds(pl.multiple_of(who * chunk, 8), chunk)

    barrier = pltpu.get_barrier_semaphore()
    for d in range(1, count):
        pl.semaphore_signal(barrier, inc=1, device_id={"space": (me + d) % count}, device_id_type=MESH)
    if turns > 1:
        pl.semaphore_signal(barrier, inc=1, device_id={"seg": sooner}, device_id_type=MESH)
    pl.semaphore_wait(barrier, count - 1 + (turns > 1))

    maps, vectors = [], []
    for d in range(1, count):
        target = (me + d) % count
        copy = pltpu.make_async_remote_copy(
            src_ref=mats_ref.at[share(target)], dst_ref=land_ref.at[d],
            send_sem=send_m.at[d], recv_sem=recv_m.at[d],
            device_id={"space": target}, device_id_type=MESH,
        )
        copy.start()
        maps.append(copy)
    for d in range(1, count):
        target = (me + d) % count
        copy = pltpu.make_async_remote_copy(
            src_ref=vecs_ref, dst_ref=vland_ref.at[d],
            send_sem=send_v.at[d], recv_sem=recv_v.at[d],
            device_id={"space": target}, device_id_type=MESH,
        )
        copy.start()
        vectors.append(copy)
    total = mats_ref[share(me), :]
    for d in range(1, count):
        maps[d - 1].wait_recv()
        total = total + land_ref[d]
    sum_ref[...] = total
    gathers = []
    for d in range(1, count):
        copy = pltpu.make_async_remote_copy(
            src_ref=sum_ref, dst_ref=all_ref.at[share(me)],
            send_sem=send_a.at[d], recv_sem=recv_a.at[d],
            device_id={"space": (me + d) % count}, device_id_type=MESH,
        )
        copy.start()
        gathers.append(copy)
    all_ref[share(me), :] = total
    vland_ref[0] = vecs_ref[...]
    for copy in vectors:
        copy.wait_recv()
    vecs = jnp.zeros((segs, nm), F32)
    for who in range(count):
        vecs = vecs + vland_ref[(me + count - who) % count]
    for d in range(1, count):
        source = (me + count - d) % count
        pltpu.make_async_remote_copy(
            src_ref=sum_ref, dst_ref=all_ref.at[share(source)],
            send_sem=send_a.at[d], recv_sem=recv_a.at[d],
            device_id={"space": (me + d) % count}, device_id_type=MESH,
        ).wait_recv()

    def chain(current, keep):
        for s in range(segs):
            if keep:
                coeffs_ref[s : s + 1, :] = current[0:1, :]
            if not keep or s < segs - 1:
                current = dot_turned(current, all_ref[s * nm : (s + 1) * nm, :], 1, HI) + vecs[s : s + 1, :]
        return current

    current = jnp.zeros((8, nm), F32)
    for step in range(turns - 1):
        end_ref[step] = chain(current, False)
        copy = pltpu.make_async_remote_copy(
            src_ref=end_ref.at[step], dst_ref=start_ref.at[step],
            send_sem=send_s.at[step], recv_sem=recv_s.at[step],
            device_id={"seg": later}, device_id_type=MESH,
        )
        copy.start()
        copy.wait()
        current = jnp.where(turn == 0, 0.0, start_ref[step])
    chain(current, True)
    for copy in maps + vectors + gathers:
        copy.wait_send()


def selectors():
    sel = np.zeros((8, 9, 256), np.float32)
    rep = np.zeros((8, 256), np.float32)
    for i in range(3):
        for w in range(10):
            for g in range(8):
                lane = 80 * i + 8 * w + g
                rep[g, lane] = 1.0
                for col in range(8):
                    if 0 <= w - col < 3:
                        sel[col, 3 * i + w - col, lane] = 1.0
    return sel, rep, jnp.asarray(np.tile(np.eye(64, dtype=np.float32), (1, 4)), BF16)


VM = pl.BlockSpec(memory_space=pltpu.VMEM)
MESH = pl.DeviceIdType.MESH
SM = pl.BlockSpec(memory_space=pltpu.SMEM)


def on_device(
    modes, states, lift_one, kern_one, bias_one, proj_one, lift_two, kern_two, bias_two, proj_two
):
    fields, rows, cols, nmodes = modes.shape
    segs = states.shape[0]
    channels = lift_one.shape[0]
    count = lax.axis_size("space")
    down = [(i, i + 1) for i in range(count - 1)]
    up = [(i + 1, i) for i in range(count - 1)]

    before = lax.ppermute(states[:, :, rows - 2 :], "space", down)
    after = lax.ppermute(states[:, :, :2], "space", up)
    turns = lax.axis_size("seg")
    follow = lax.ppermute(states[0], "seg", [(i + 1, i) for i in range(turns - 1)])

    own = jnp.transpose(modes, (1, 2, 0, 3)).reshape(rows, cols * fields, nmodes)
    turned = jnp.transpose(own, (0, 2, 1))
    own = jnp.pad(own, ((0, 0), (8, 24), (0, 0)))
    low = lax.ppermute(own[rows - 2 :], "space", down)
    high = lax.ppermute(own[:2], "space", up)

    extended = jnp.concatenate([before, states, after], axis=2)
    u = jnp.transpose(extended, (2, 3, 0, 1)).reshape(rows + 4, cols * segs, fields)
    glob = lax.axis_index("space") * rows - 1 + jnp.arange(rows + 2)
    mask = ((glob >= 0) & (glob < rows * count)).astype(F32)

    groups = cols // 4
    span = cols * segs
    slope_one, slope_two, final = pl.pallas_call(
        functools.partial(advance_kernel, rows),
        out_shape=(
            jax.ShapeDtypeStruct((rows + 2, groups, segs, 4 * channels), F32),
            jax.ShapeDtypeStruct((rows, groups, segs, 4 * channels), F32),
            jax.ShapeDtypeStruct((rows, span, fields), F32),
        ),
        in_specs=[SM] + [VM] * 9,
        out_specs=(VM, VM, VM),
        scratch_shapes=[
            pltpu.VMEM((rows + 4, span + 16, channels), F32),
            pltpu.VMEM((rows + 2, span + 16, channels), F32),
            pltpu.VMEM((rows + 2, span, fields), F32),
        ],
        compiler_params=pltpu.CompilerParams(vmem_limit_bytes=56 * 2**20),
        cost_estimate=pl.CostEstimate(flops=10**8, bytes_accessed=10**7, transcendentals=10**6),
    )(
        mask, u, lift_one.T, lift_two.T, proj_one, proj_two, kern_one.T, kern_two.T,
        bias_one[None], bias_two[None],
    )
    advanced = jnp.transpose(final.reshape(rows, cols, segs, fields), (2, 3, 0, 1))
    defects = (advanced - jnp.concatenate([states[1:], follow[None]], axis=0)).astype(BF16)
    vecs = jnp.einsum("sfrw,frwk->sk", defects, modes, preferred_element_type=F32)

    sel, rep, spread = selectors()
    lines = cols * fields
    mats = pl.pallas_call(
        functools.partial(tangent_kernel, rows, segs),
        out_shape=jax.ShapeDtypeStruct((segs * nmodes, nmodes), F32),
        in_specs=[VM] * 15,
        out_specs=VM,
        scratch_shapes=[
            pltpu.VMEM((rows + 4, lines + 32, nmodes), BF16),
            pltpu.VMEM((rows + 2, lines + 32, segs * nmodes), F32),
            pltpu.VMEM((lines, segs * nmodes), BF16),
            pltpu.VMEM((2, 256, 256), BF16),
            pltpu.VMEM((2, 256, 256), BF16),
            pltpu.VMEM((32, 256), F32),
            pltpu.VMEM((32, 256), F32),
        ],
        compiler_params=pltpu.CompilerParams(vmem_limit_bytes=56 * 2**20),
        cost_estimate=pl.CostEstimate(flops=2 * 10**10, bytes_accessed=10**7, transcendentals=0),
    )(
        low, own, high, turned, slope_one, slope_two, proj_one, proj_two, kern_one.T, kern_two.T,
        lift_one.T, lift_two.T, sel, rep, spread,
    )

    chunk = segs * nmodes // count
    dma = pltpu.SemaphoreType.DMA
    coeffs = pl.pallas_call(
        functools.partial(close_kernel, segs, count, turns),
        out_shape=jax.ShapeDtypeStruct((segs, nmodes), F32),
        in_specs=[VM] * 2,
        out_specs=VM,
        scratch_shapes=[
            pltpu.VMEM((count, chunk, nmodes), F32),
            pltpu.VMEM((chunk, nmodes), F32),
            pltpu.VMEM((segs * nmodes, nmodes), F32),
            pltpu.VMEM((count, segs, nmodes), F32),
            pltpu.VMEM((turns, 8, nmodes), F32),
            pltpu.VMEM((turns, 8, nmodes), F32),
            dma((count,)), dma((count,)), dma((count,)), dma((count,)), dma((count,)), dma((count,)),
            dma((turns,)), dma((turns,)),
        ],
        compiler_params=pltpu.CompilerParams(collective_id=0, has_side_effects=True),
    )(mats, vecs)
    return advanced, coeffs


def solution(mesh):
    placed = (
        P(None, "space", None, None),
        P(("groups", "seg"), None, "space", None),
        P(), P(), P(), P(), P(), P(), P(), P(),
    )
    return jax.shard_map(
        on_device,
        mesh=mesh,
        in_specs=placed,
        out_specs=(P(("groups", "seg"), None, "space", None), P(("groups", "seg"), None)),
        check_vma=False,
    )
```
